32 devices in a mesh: aux: 4 (over y, x), basis: 8 (over z, core).
Axes of the slice: x: 2, y: 2, z: 4, core: 2. Of those that a mesh axis runs over, the one named last changes fastest.
Arguments:
- factors: bfloat16 [16, 500, 8192], P('aux', None, 'basis'), may hold values from -0.125 to 0.125
Outputs:
- exchange_band: float32 [3, 8192, 1024], P(None, ('basis', 'aux'))
The draws below stay inside these ranges and needn't reach their ends.
All inputs are finite; a program needn't handle non-finite values.
Results may differ from the reference program's by a relative error of at most 0.0003.
Values may be sent and summed in bfloat16 or wider, within the bound.
A program may use at most 64 MiB of HBM per device.

```python
import jax
import jax.numpy as jnp
from jax import lax

NBF = 8192
NOCC = 500
P_DEV = 4
SHIFTS = 3
NAUX = 16
N_AUX = 4
N_BASIS = 8


def with_spikes(array, key, source, target, blocks, factor):
    def block_of(dim):
        return (jnp.arange(array.shape[dim]) // (array.shape[dim] // blocks)).reshape((-1,) + (1,) * (array.ndim - 1 - dim))

    near = jax.random.permutation(key, blocks)[block_of(target)]
    far = (block_of(target) + blocks // 2) % blocks
    return jnp.where((block_of(source) == near) | (block_of(source) == far), factor * array, array)


def block_levels(own_key, shape, cuts, smallest, top_value):
    gain, own = 1.0, jax.random.fold_in(own_key, 6)
    for dim, blocks in cuts:
        draws = jnp.exp(jax.random.uniform(jax.random.fold_in(own, dim), (blocks,), jnp.float32, smallest / len(cuts), top_value / len(cuts)))
        gain = gain * jnp.repeat(draws, shape[dim] // blocks).reshape([-1 if axis == dim else 1 for axis in range(len(shape))])
    return gain


def noise_with(own_key, shape, spread, most, cuts, heavy, held_as=jnp.bfloat16):
    result = spread * jax.random.normal(own_key, shape, jnp.float32)
    if cuts:
        result = result * block_levels(own_key, shape, cuts, -0.22, 0.18)
    return jnp.clip(with_spikes(result, jax.random.fold_in(own_key, 3), *heavy), -most, most).astype(held_as)


def setup_inputs(seed: int = 0) -> dict:
    seeds = jax.random.split(jax.random.key(seed), 2)
    return {
        "factors": noise_with(seeds[0], (NAUX, NOCC, NBF), (NOCC * 8) ** -0.5, 0.125, ((0, 4), (2, 8)), (0, 2, 8, 2.0)),
    }


def reference(factors):
    block = NBF // N_BASIS
    grouped = factors.reshape(N_AUX, P_DEV * NOCC, NBF)

    def one_block(index):
        def one_group(total, flat):
            own = lax.dynamic_slice_in_dim(flat, (index * block).astype(jnp.int32), block, 1)
            tiles = []
            for s in range(SHIFTS):
                other_index = (index + s) % N_BASIS
                other = lax.dynamic_slice_in_dim(flat, (other_index * block).astype(jnp.int32), block, 1)
                part = lax.dot_general(own, other, (((0,), (0,)), ((), ())), preferred_element_type=jnp.float32)
                tiles.append(part)
            return total + jnp.stack(tiles), None

        start = jnp.zeros((SHIFTS, block, block), jnp.float32)
        total, _ = lax.scan(one_group, start, grouped)
        return total

    stacked = lax.map(one_block, jnp.arange(N_BASIS, dtype=jnp.int32))
    return jnp.transpose(stacked, (1, 0, 2, 3)).reshape(SHIFTS, NBF, block)
```

```python
import functools

import jax
import jax.numpy as jnp
from jax import lax
from jax.experimental import pallas as pl
from jax.experimental.pallas import tpu as pltpu
from jax.sharding import PartitionSpec as P

SHIFTS = 3
MESH = pl.DeviceIdType.MESH


def round_up(value, step):
    return -(-value // step) * step


def kernel(cfg, x_ref, out_ref, own_t, got, part, *rest):
    depth, full, block, width, chunks, bits, n_aux, n_basis = cfg
    hop_refs = rest[: 2 * bits]
    ring_send, ring_recv, hop_send, hop_recv = rest[2 * bits :]
    half = width // 2
    rows = block // n_aux
    me_aux = lax.axis_index("aux")
    me_basis = lax.axis_index("basis")
    left = lax.rem(me_basis + n_basis - 1, n_basis)
    right = lax.rem(me_basis + 1, n_basis)
    my_bit = [lax.rem(me_aux // (2**q), 2) for q in range(bits)]
    partner = [me_aux + (1 - 2 * my_bit[q]) * 2**q for q in range(bits)]

    barrier = pltpu.get_barrier_semaphore()
    for who in [{"basis": left}, {"basis": right}] + [{"aux": p} for p in partner]:
        pl.semaphore_signal(barrier, inc=1, device_id=who, device_id_type=MESH)
    if full > depth:
        for s in range(SHIFTS - 1):
            got[s, depth:full, :] = jnp.zeros((full - depth, block), got.dtype)
    pl.semaphore_wait(barrier, 2 + bits)

    def ring_copy(s, j):
        cols = pl.ds(j * width, width)
        source = x_ref if s == 0 else got.at[s - 1]
        return pltpu.make_async_remote_copy(
            src_ref=source.at[pl.ds(0, depth), cols],
            dst_ref=got.at[s, pl.ds(0, depth), cols],
            send_sem=ring_send.at[s, j],
            recv_sem=ring_recv.at[s, j],
            device_id={"basis": left},
            device_id_type=MESH,
        )

    def order(side):
        return list(range(bits)) if side == 0 else list(range(bits))[::-1]

    def cut(side, hop, last):
        index = [pl.ds(0, 2)] * bits
        for step, q in enumerate(order(side)[: hop + 1]):
            index[bits - 1 - q] = my_bit[q] if step < hop or not last else 1 - my_bit[q]
        return tuple(index)

    def hop_copy(n, side, hop):
        q = order(side)[hop]
        return pltpu.make_async_remote_copy(
            src_ref=part.at[(n, side) + cut(side, hop, True)],
            dst_ref=hop_refs[side * bits + hop].at[n],
            send_sem=hop_send.at[n, side, hop],
            recv_sem=hop_recv.at[n, side, hop],
            device_id={"aux": partner[q]},
            device_id_type=MESH,
        )

    for j in range(chunks):
        ring_copy(0, j).start()

    step_cols = 128
    for i in range(block // step_cols):
        cols = pl.ds(i * step_cols, step_cols)
        own_t[cols, :] = x_ref[:, cols].T

    tiles = [(s, j) for s in range(SHIFTS) for j in range(chunks)]
    lhs_rows = min(256, block)

    def compute(n):
        s, j = tiles[n]
        cols = pl.ds(j * width, width)

        def body(i, carry):
            here = pl.ds(pl.multiple_of(i * lhs_rows, lhs_rows), lhs_rows)
            other = x_ref[:, cols] if s == 0 else got[s - 1, :, cols]
            product = jnp.dot(
                own_t[here, :], other, preferred_element_type=jnp.float32
            )
            per = lhs_rows // rows
            for r in range(per):
                g = i * per + r
                index = [lax.rem(g // (2**q), 2) for q in range(bits)][::-1]
                for side in range(2):
                    part[(n, side) + tuple(index)] = product[
                        r * rows : (r + 1) * rows, side * half : (side + 1) * half
                    ]
            return carry

        lax.fori_loop(0, block // lhs_rows, body, 0)

    def finish(n, hop):
        s, j = tiles[n]
        for side in range(2):
            hop_copy(n, side, hop).wait_recv()
            index = (n, side) + cut(side, hop, False)
            total = part[index] + hop_refs[side * bits + hop][n]
            if hop < bits - 1:
                part[index] = total
                hop_copy(n, side, hop + 1).start()
            else:
                out_ref[s, :, j * width + side * half : j * width + (side + 1) * half] = total

    count = len(tiles)
    lag = 2
    for n in range(count + lag * bits):
        if n < count:
            s, j = tiles[n]
            if s > 0:
                ring_copy(s - 1, j).wait_recv()
                if s < SHIFTS - 1:
                    ring_copy(s, j).start()
            compute(n)
            for side in range(2):
                hop_copy(n, side, 0).start()
        for hop in range(bits):
            m = n - lag * (hop + 1)
            if 0 <= m < count:
                finish(m, hop)

    for s in range(SHIFTS - 1):
        for j in range(chunks):
            ring_copy(s, j).wait_send()
    for n in range(count):
        for side in range(2):
            for hop in range(bits):
                hop_copy(n, side, hop).wait_send()


def on_device(n_aux, n_basis, factors):
    depth = factors.shape[0] * factors.shape[1]
    block = factors.shape[2]
    full = round_up(depth, 256)
    flat = jnp.pad(factors.reshape(depth, block), ((0, full - depth), (0, 0)))
    bits = n_aux.bit_length() - 1
    width = 256
    chunks = block // width
    count = SHIFTS * chunks
    rows = block // n_aux
    half = width // 2
    hop_bufs = []
    for side in range(2):
        for hop in range(bits):
            shape = (count,) + (2,) * (bits - 1 - hop) + (rows, half)
            hop_bufs.append(pltpu.VMEM(shape, jnp.float32))
    cfg = (depth, full, block, width, chunks, bits, n_aux, n_basis)
    return pl.pallas_call(
        functools.partial(kernel, cfg),
        out_shape=jax.ShapeDtypeStruct((SHIFTS, rows, block), jnp.float32),
        in_specs=[pl.BlockSpec(memory_space=pltpu.VMEM)],
        out_specs=pl.BlockSpec(memory_space=pltpu.VMEM),
        scratch_shapes=[
            pltpu.VMEM((block, full), jnp.bfloat16),
            pltpu.VMEM((SHIFTS - 1, full, block), jnp.bfloat16),
            pltpu.VMEM((count, 2) + (2,) * bits + (rows, half), jnp.float32),
            *hop_bufs,
            pltpu.SemaphoreType.DMA((SHIFTS - 1, chunks)),
            pltpu.SemaphoreType.DMA((SHIFTS - 1, chunks)),
            pltpu.SemaphoreType.DMA((count, 2, bits)),
            pltpu.SemaphoreType.DMA((count, 2, bits)),
        ],
        compiler_params=pltpu.CompilerParams(
            collective_id=0, has_side_effects=True, vmem_limit_bytes=58 * 2**20
        ),
        cost_estimate=pl.CostEstimate(
            flops=2 * SHIFTS * full * block * block,
            bytes_accessed=2 * full * block + 4 * SHIFTS * rows * block,
            transcendentals=0,
        ),
    )(flat)


def solution(mesh):
    n_aux, n_basis = mesh.shape["aux"], mesh.shape["basis"]
    return jax.shard_map(
        functools.partial(on_device, n_aux, n_basis),
        mesh=mesh,
        in_specs=(P("aux", None, "basis"),),
        out_specs=P(None, ("basis", "aux"), None),
        check_vma=False,
    )
```

```python
import functools

import jax
import jax.numpy as jnp
from jax import lax
from jax.experimental import pallas as pl
from jax.experimental.pallas import tpu as pltpu
from jax.sharding import PartitionSpec as P

SHIFTS = 3
MESH = pl.DeviceIdType.MESH


def round_up(value, step):
    return -(-value // step) * step


def kernel(cfg, x_hbm, out_ref, x_ref, own_t, got, part, *rest):
    depth, full, block, width, chunks, bits, n_aux, n_basis = cfg
    hop_refs = rest[: 2 * bits]
    load_sem, ring_send, ring_recv, hop_send, hop_recv = rest[2 * bits :]
    half = width // 2
    rows = block // n_aux
    me_aux = lax.axis_index("aux")
    me_basis = lax.axis_index("basis")
    left = lax.rem(me_basis + n_basis - 1, n_basis)
    right = lax.rem(me_basis + 1, n_basis)
    my_bit = [lax.rem(me_aux // (2**q), 2) for q in range(bits)]
    partner = [me_aux + (1 - 2 * my_bit[q]) * 2**q for q in range(bits)]

    def load(j):
        here = (pl.ds(0, depth), pl.ds(j * width, width))
        return pltpu.make_async_copy(x_hbm.at[here], x_ref.at[here], load_sem.at[j])

    for j in range(chunks):
        load(j).start()

    barrier = pltpu.get_barrier_semaphore()
    for who in [{"basis": left}, {"basis": right}] + [{"aux": p} for p in partner]:
        pl.semaphore_signal(barrier, inc=1, device_id=who, device_id_type=MESH)
    if full > depth:
        for s in range(SHIFTS - 1):
            got[s, depth:full, :] = jnp.zeros((full - depth, block), got.dtype)
        x_ref[depth:full, :] = jnp.zeros((full - depth, block), x_ref.dtype)
    pl.semaphore_wait(barrier, 2 + bits)

    def ring_copy(s, j):
        cols = pl.ds(j * width, width)
        source = x_ref if s == 0 else got.at[s - 1]
        return pltpu.make_async_remote_copy(
            src_ref=source.at[pl.ds(0, depth), cols],
            dst_ref=got.at[s, pl.ds(0, depth), cols],
            send_sem=ring_send.at[s, j],
            recv_sem=ring_recv.at[s, j],
            device_id={"basis": left},
            device_id_type=MESH,
        )

    def order(side):
        return list(range(bits)) if side == 0 else list(range(bits))[::-1]

    def cut(side, hop, last):
        index = [pl.ds(0, 2)] * bits
        for step, q in enumerate(order(side)[: hop + 1]):
            index[bits - 1 - q] = my_bit[q] if step < hop or not last else 1 - my_bit[q]
        return tuple(index)

    def hop_copy(n, side, hop):
        q = order(side)[hop]
        return pltpu.make_async_remote_copy(
            src_ref=part.at[(n, side) + cut(side, hop, True)],
            dst_ref=hop_refs[side * bits + hop].at[n],
            send_sem=hop_send.at[n, side, hop],
            recv_sem=hop_recv.at[n, side, hop],
            device_id={"aux": partner[q]},
            device_id_type=MESH,
        )

    for j in range(chunks):
        load(j).wait()
        ring_copy(0, j).start()

    step_cols = 128
    for i in range(block // step_cols):
        cols = pl.ds(i * step_cols, step_cols)
        own_t[cols, :] = x_ref[:, cols].T

    tiles = [(s, j) for s in range(SHIFTS) for j in range(chunks)]
    lhs_rows = min(256, block)

    def compute(n):
        s, j = tiles[n]
        cols = pl.ds(j * width, width)

        def body(i, carry):
            here = pl.ds(pl.multiple_of(i * lhs_rows, lhs_rows), lhs_rows)
            other = x_ref[:, cols] if s == 0 else got[s - 1, :, cols]
            product = jnp.dot(
                own_t[here, :], other, preferred_element_type=jnp.float32
            )
            per = lhs_rows // rows
            for r in range(per):
                g = i * per + r
                index = [lax.rem(g // (2**q), 2) for q in range(bits)][::-1]
                for side in range(2):
                    part[(n, side) + tuple(index)] = product[
                        r * rows : (r + 1) * rows, side * half : (side + 1) * half
                    ]
            return carry

        lax.fori_loop(0, block // lhs_rows, body, 0)

    def finish(n, hop):
        s, j = tiles[n]
        for side in range(2):
            hop_copy(n, side, hop).wait_recv()
            index = (n, side) + cut(side, hop, False)
            total = part[index] + hop_refs[side * bits + hop][n]
            if hop < bits - 1:
                part[index] = total
                hop_copy(n, side, hop + 1).start()
            else:
                out_ref[s, :, j * width + side * half : j * width + (side + 1) * half] = total

    count = len(tiles)
    lag = 2
    for n in range(count + lag * bits):
        if n < count:
            s, j = tiles[n]
            if s > 0:
                ring_copy(s - 1, j).wait_recv()
                if s < SHIFTS - 1:
                    ring_copy(s, j).start()
            compute(n)
            for side in range(2):
                hop_copy(n, side, 0).start()
        for hop in range(bits):
            m = n - lag * (hop + 1)
            if 0 <= m < count:
                finish(m, hop)

    for s in range(SHIFTS - 1):
        for j in range(chunks):
            ring_copy(s, j).wait_send()
    for n in range(count):
        for side in range(2):
            for hop in range(bits):
                hop_copy(n, side, hop).wait_send()


def on_device(n_aux, n_basis, factors):
    depth = factors.shape[0] * factors.shape[1]
    block = factors.shape[2]
    full = round_up(depth, 256)
    flat = jnp.transpose(factors, (1, 0, 2)).reshape(depth, block)
    bits = n_aux.bit_length() - 1
    width = 256
    chunks = block // width
    count = SHIFTS * chunks
    rows = block // n_aux
    half = width // 2
    hop_bufs = []
    for side in range(2):
        for hop in range(bits):
            shape = (count,) + (2,) * (bits - 1 - hop) + (rows, half)
            hop_bufs.append(pltpu.VMEM(shape, jnp.float32))
    cfg = (depth, full, block, width, chunks, bits, n_aux, n_basis)
    return pl.pallas_call(
        functools.partial(kernel, cfg),
        out_shape=jax.ShapeDtypeStruct((SHIFTS, rows, block), jnp.float32),
        in_specs=[pl.BlockSpec(memory_space=pl.ANY)],
        out_specs=pl.BlockSpec(memory_space=pltpu.VMEM),
        scratch_shapes=[
            pltpu.VMEM((full, block), jnp.bfloat16),
            pltpu.VMEM((block, full), jnp.bfloat16),
            pltpu.VMEM((SHIFTS - 1, full, block), jnp.bfloat16),
            pltpu.VMEM((count, 2) + (2,) * bits + (rows, half), jnp.float32),
            *hop_bufs,
            pltpu.SemaphoreType.DMA((chunks,)),
            pltpu.SemaphoreType.DMA((SHIFTS - 1, chunks)),
            pltpu.SemaphoreType.DMA((SHIFTS - 1, chunks)),
            pltpu.SemaphoreType.DMA((count, 2, bits)),
            pltpu.SemaphoreType.DMA((count, 2, bits)),
        ],
        compiler_params=pltpu.CompilerParams(
            collective_id=0, has_side_effects=True, vmem_limit_bytes=58 * 2**20
        ),
        cost_estimate=pl.CostEstimate(
            flops=2 * SHIFTS * full * block * block,
            bytes_accessed=2 * full * block + 4 * SHIFTS * rows * block,
            transcendentals=0,
        ),
    )(flat)


def solution(mesh):
    n_aux, n_basis = mesh.shape["aux"], mesh.shape["basis"]
    return jax.shard_map(
        functools.partial(on_device, n_aux, n_basis),
        mesh=mesh,
        in_specs=(P("aux", None, "basis"),),
        out_specs=P(None, ("basis", "aux"), None),
        check_vma=False,
    )
```

```python
import functools

import jax
import jax.numpy as jnp
from jax import lax
from jax.experimental import pallas as pl
from jax.experimental.pallas import tpu as pltpu
from jax.sharding import PartitionSpec as P

SHIFTS = 3
SMALLEST = 2.0**-125
UNIT_ROWS = 16
MESH = pl.DeviceIdType.MESH


def round_up(value, step):
    return -(-value // step) * step


def encode(value, unit):
    scaled = value * (1.0 / unit)
    power = scaled * scaled
    power = power * power
    power = power * power
    return jnp.where(scaled < 0, -power, power).astype(jnp.bfloat16)


def decode(code, unit):
    code = code.astype(jnp.float32)
    fourth = lax.rsqrt(lax.rsqrt(jnp.maximum(jnp.abs(code), SMALLEST)))
    root = fourth * lax.rsqrt(fourth)
    root = jnp.where(code > 0, root, jnp.where(code < 0, -root, 0.0))
    return root * unit


def kernel(cfg, x_hbm, out_ref, x_ref, own_t, got, part, code_out, code_in, *rest):
    depth, full, block, width, chunks, bits, n_aux, n_basis = cfg
    later = bits - 1
    hop_refs = rest[: 2 * later]
    load_sem, ring_send, ring_recv, hop_send, hop_recv = rest[2 * later :]
    half = width // 2
    rows = block // n_aux
    me_aux = lax.axis_index("aux")
    me_basis = lax.axis_index("basis")
    left = lax.rem(me_basis + n_basis - 1, n_basis)
    right = lax.rem(me_basis + 1, n_basis)
    my_bit = [lax.rem(me_aux // (2**q), 2) for q in range(bits)]
    partner = [me_aux + (1 - 2 * my_bit[q]) * 2**q for q in range(bits)]

    def load(j):
        here = (pl.ds(0, depth), pl.ds(j * width, width))
        return pltpu.make_async_copy(x_hbm.at[here], x_ref.at[here], load_sem.at[j])

    for j in range(chunks):
        load(j).start()

    barrier = pltpu.get_barrier_semaphore()
    for who in [{"basis": left}, {"basis": right}] + [{"aux": p} for p in partner]:
        pl.semaphore_signal(barrier, inc=1, device_id=who, device_id_type=MESH)
    if full > depth:
        for s in range(SHIFTS - 1):
            got[s, depth:full, :] = jnp.zeros((full - depth, block), got.dtype)
        x_ref[depth:full, :] = jnp.zeros((full - depth, block), x_ref.dtype)
    pl.semaphore_wait(barrier, 2 + bits)

    def ring_copy(s, j):
        cols = pl.ds(j * width, width)
        source = x_ref if s == 0 else got.at[s - 1]
        return pltpu.make_async_remote_copy(
            src_ref=source.at[pl.ds(0, depth), cols],
            dst_ref=got.at[s, pl.ds(0, depth), cols],
            send_sem=ring_send.at[s, j],
            recv_sem=ring_recv.at[s, j],
            device_id={"basis": left},
            device_id_type=MESH,
        )

    def order(side):
        return list(range(bits)) if side == 0 else list(range(bits))[::-1]

    def cut(side, hop, last):
        index = [pl.ds(0, 2)] * bits
        for step, q in enumerate(order(side)[: hop + 1]):
            index[bits - 1 - q] = my_bit[q] if step < hop or not last else 1 - my_bit[q]
        return tuple(index)

    def hop_copy(n, side, hop):
        q = order(side)[hop]
        if hop == 0:
            source, target = code_out.at[n, side], code_in.at[n, side]
        else:
            source = part.at[(n, side) + cut(side, hop, True)]
            target = hop_refs[side * later + hop - 1].at[n]
        return pltpu.make_async_remote_copy(
            src_ref=source,
            dst_ref=target,
            send_sem=hop_send.at[n, side, hop],
            recv_sem=hop_recv.at[n, side, hop],
            device_id={"aux": partner[q]},
            device_id_type=MESH,
        )

    for j in range(chunks):
        load(j).wait()
        ring_copy(0, j).start()

    step_cols = 128
    for i in range(block // step_cols):
        cols = pl.ds(i * step_cols, step_cols)
        own_t[cols, :] = x_ref[:, cols].T

    tiles = [(s, j) for s in range(SHIFTS) for j in range(chunks)]
    lhs_rows = min(256, block)
    sent = block // 2

    def compute(n):
        s, j = tiles[n]
        cols = pl.ds(j * width, width)

        def body(i, carry):
            here = pl.ds(pl.multiple_of(i * lhs_rows, lhs_rows), lhs_rows)
            other = x_ref[:, cols] if s == 0 else got[s - 1, :, cols]
            product = jnp.dot(
                own_t[here, :], other, preferred_element_type=jnp.float32
            )
            per = lhs_rows // rows
            for r in range(per):
                g = i * per + r
                index = [lax.rem(g // (2**q), 2) for q in range(bits)][::-1]
                for side in range(2):
                    part[(n, side) + tuple(index)] = product[
                        r * rows : (r + 1) * rows, side * half : (side + 1) * half
                    ]
            size = jnp.abs(product).reshape(lhs_rows // 8, 8, width)
            return jnp.maximum(carry, jnp.max(size, axis=0))

        start = jnp.zeros((8, width), jnp.float32)
        most = jnp.max(lax.fori_loop(0, block // lhs_rows, body, start))
        unit = jnp.maximum(most, 2.0**-90) * 2.0**-14
        for side in range(2):
            tail = (n, side, pl.ds(sent, UNIT_ROWS))
            code_out[tail] = jnp.full((UNIT_ROWS, half), unit).astype(jnp.bfloat16)
            used = code_out[tail].astype(jnp.float32)[0:1]
            value = part[(n, side) + cut(side, 0, True)].reshape(sent, half)
            code_out[n, side, 0:sent] = encode(value, used)
            hop_copy(n, side, 0).start()

    def finish(n, hop):
        s, j = tiles[n]
        for side in range(2):
            hop_copy(n, side, hop).wait_recv()
            index = (n, side) + cut(side, hop, False)
            if hop == 0:
                unit = code_in[n, side, sent:].astype(jnp.float32)[0:1]
                arrived = decode(code_in[n, side, 0:sent], unit)
                arrived = arrived.reshape((2,) * (bits - 1) + (rows, half))
            else:
                arrived = hop_refs[side * later + hop - 1][n]
            total = part[index] + arrived
            if hop < bits - 1:
                part[index] = total
                hop_copy(n, side, hop + 1).start()
            else:
                out_ref[s, :, j * width + side * half : j * width + (side + 1) * half] = total

    count = len(tiles)
    done = {}

    def catch_up(last, lag):
        for hop in range(bits):
            for m in range(done.get(hop, 0), max(last - lag * hop + 1, 0)):
                finish(m, hop)
                done[hop] = m + 1

    for n in range(count):
        s, j = tiles[n]
        if s > 0:
            catch_up(n - 1, 0)
            ring_copy(s - 1, j).wait_recv()
            if s < SHIFTS - 1:
                ring_copy(s, j).start()
        compute(n)
        if s == 0:
            catch_up(n - 1, 1)
    catch_up(count - 1, 0)

    for s in range(SHIFTS - 1):
        for j in range(chunks):
            ring_copy(s, j).wait_send()
    for n in range(count):
        for side in range(2):
            for hop in range(bits):
                hop_copy(n, side, hop).wait_send()


def on_device(n_aux, n_basis, factors):
    depth = factors.shape[0] * factors.shape[1]
    block = factors.shape[2]
    full = round_up(depth, 256)
    flat = jnp.transpose(factors, (1, 0, 2)).reshape(depth, block)
    bits = n_aux.bit_length() - 1
    width = 256
    chunks = block // width
    count = SHIFTS * chunks
    rows = block // n_aux
    half = width // 2
    hop_bufs = []
    for side in range(2):
        for hop in range(1, bits):
            shape = (count,) + (2,) * (bits - 1 - hop) + (rows, half)
            hop_bufs.append(pltpu.VMEM(shape, jnp.float32))
    cfg = (depth, full, block, width, chunks, bits, n_aux, n_basis)
    return pl.pallas_call(
        functools.partial(kernel, cfg),
        out_shape=jax.ShapeDtypeStruct((SHIFTS, rows, block), jnp.float32),
        in_specs=[pl.BlockSpec(memory_space=pl.ANY)],
        out_specs=pl.BlockSpec(memory_space=pltpu.VMEM),
        scratch_shapes=[
            pltpu.VMEM((full, block), jnp.bfloat16),
            pltpu.VMEM((block, full), jnp.bfloat16),
            pltpu.VMEM((SHIFTS - 1, full, block), jnp.bfloat16),
            pltpu.VMEM((count, 2) + (2,) * bits + (rows, half), jnp.float32),
            pltpu.VMEM((count, 2, block // 2 + UNIT_ROWS, half), jnp.bfloat16),
            pltpu.VMEM((count, 2, block // 2 + UNIT_ROWS, half), jnp.bfloat16),
            *hop_bufs,
            pltpu.SemaphoreType.DMA((chunks,)),
            pltpu.SemaphoreType.DMA((SHIFTS - 1, chunks)),
            pltpu.SemaphoreType.DMA((SHIFTS - 1, chunks)),
            pltpu.SemaphoreType.DMA((count, 2, bits)),
            pltpu.SemaphoreType.DMA((count, 2, bits)),
        ],
        compiler_params=pltpu.CompilerParams(
            collective_id=0, has_side_effects=True, vmem_limit_bytes=58 * 2**20
        ),
        cost_estimate=pl.CostEstimate(
            flops=2 * SHIFTS * full * block * block,
            bytes_accessed=2 * full * block + 4 * SHIFTS * rows * block,
            transcendentals=0,
        ),
    )(flat)


def solution(mesh):
    n_aux, n_basis = mesh.shape["aux"], mesh.shape["basis"]
    return jax.shard_map(
        functools.partial(on_device, n_aux, n_basis),
        mesh=mesh,
        in_specs=(P("aux", None, "basis"),),
        out_specs=P(None, ("basis", "aux"), None),
        check_vma=False,
    )
```

```python
import functools

import jax
import jax.numpy as jnp
from jax import lax
from jax.experimental import pallas as pl
from jax.experimental.pallas import tpu as pltpu
from jax.sharding import PartitionSpec as P

SHIFTS = 3
AHEAD = 3
SMALLEST = 2.0**-125
UNIT_ROWS = 16
MESH = pl.DeviceIdType.MESH


def round_up(value, step):
    return -(-value // step) * step


def encode(value, unit):
    scaled = value * (1.0 / unit)
    power = scaled * scaled
    power = power * power
    power = power * power
    return jnp.where(scaled < 0, -power, power).astype(jnp.bfloat16)


def decode(code, unit):
    code = code.astype(jnp.float32)
    fourth = lax.rsqrt(lax.rsqrt(jnp.maximum(jnp.abs(code), SMALLEST)))
    root = fourth * lax.rsqrt(fourth)
    root = jnp.where(code > 0, root, jnp.where(code < 0, -root, 0.0))
    return root * unit


def kernel(cfg, x_hbm, out_ref, x_ref, own_t, got, part, code_out, code_in, *rest):
    depth, full, block, width, chunks, bits, n_aux, n_basis = cfg
    later = bits - 1
    hop_refs = rest[:later]
    load_sem, ring_send, ring_recv, hop_send, hop_recv = rest[later:]
    rows = block // n_aux
    me_aux = lax.axis_index("aux")
    me_basis = lax.axis_index("basis")
    left = lax.rem(me_basis + n_basis - 1, n_basis)
    right = lax.rem(me_basis + 1, n_basis)
    my_bit = [lax.rem(me_aux // (2**q), 2) for q in range(bits)]
    partner = [me_aux + (1 - 2 * my_bit[q]) * 2**q for q in range(bits)]

    def load(j):
        here = (pl.ds(0, depth), pl.ds(j * width, width))
        return pltpu.make_async_copy(x_hbm.at[here], x_ref.at[here], load_sem.at[j])

    for j in range(chunks):
        load(j).start()

    barrier = pltpu.get_barrier_semaphore()
    for who in [{"basis": left}, {"basis": right}] + [{"aux": p} for p in partner]:
        pl.semaphore_signal(barrier, inc=1, device_id=who, device_id_type=MESH)
    if full > depth:
        for s in range(SHIFTS - 1):
            got[s, depth:full, :] = jnp.zeros((full - depth, block), got.dtype)
        x_ref[depth:full, :] = jnp.zeros((full - depth, block), x_ref.dtype)
    pl.semaphore_wait(barrier, 2 + bits)

    def ring_copy(s, j):
        cols = pl.ds(j * width, width)
        source = x_ref if s == 0 else got.at[s - 1]
        return pltpu.make_async_remote_copy(
            src_ref=source.at[pl.ds(0, depth), cols],
            dst_ref=got.at[s, pl.ds(0, depth), cols],
            send_sem=ring_send.at[s, j],
            recv_sem=ring_recv.at[s, j],
            device_id={"basis": left},
            device_id_type=MESH,
        )

    def order(side):
        return list(range(bits)) if side == 0 else list(range(bits))[::-1]

    def cut(side, hop, last):
        index = [pl.ds(0, 2)] * bits
        for step, q in enumerate(order(side)[: hop + 1]):
            index[bits - 1 - q] = my_bit[q] if step < hop or not last else 1 - my_bit[q]
        return tuple(index)

    def hop_copy(n, hop):
        side = n % 2
        q = order(side)[hop]
        if hop == 0:
            source, target = code_out.at[n], code_in.at[n]
        else:
            source = part.at[(n,) + cut(side, hop, True)]
            target = hop_refs[hop - 1].at[n]
        return pltpu.make_async_remote_copy(
            src_ref=source,
            dst_ref=target,
            send_sem=hop_send.at[n, hop],
            recv_sem=hop_recv.at[n, hop],
            device_id={"aux": partner[q]},
            device_id_type=MESH,
        )

    pieces = [(s, j) for s in range(SHIFTS - 1) for j in range(chunks)]
    for j in range(chunks):
        load(j).wait()
        if j < AHEAD:
            ring_copy(*pieces[j]).start()

    step_cols = 128
    for i in range(block // step_cols):
        cols = pl.ds(i * step_cols, step_cols)
        own_t[cols, :] = x_ref[:, cols].T

    first = chunks // 2
    tiles = [(0, j) for j in range(first)]
    for i, piece in enumerate(pieces):
        tiles.append((piece[0] + 1, piece[1]))
        if first + i < chunks:
            tiles.append((0, first + i))
    lhs_rows = min(256, block)
    sent = block // 2

    def compute(n):
        s, j = tiles[n]
        cols = pl.ds(j * width, width)

        def body(i, carry):
            here = pl.ds(pl.multiple_of(i * lhs_rows, lhs_rows), lhs_rows)
            other = x_ref[:, cols] if s == 0 else got[s - 1, :, cols]
            product = jnp.dot(
                own_t[here, :], other, preferred_element_type=jnp.float32
            )
            per = lhs_rows // rows
            for r in range(per):
                g = i * per + r
                index = [lax.rem(g // (2**q), 2) for q in range(bits)][::-1]
                part[(n,) + tuple(index)] = product[r * rows : (r + 1) * rows]
            size = jnp.abs(product).reshape(lhs_rows // 8, 8, width)
            return jnp.maximum(carry, jnp.max(size, axis=0))

        start = jnp.zeros((8, width), jnp.float32)
        most = jnp.max(lax.fori_loop(0, block // lhs_rows, body, start))
        unit = jnp.maximum(most, 2.0**-90) * 2.0**-14
        tail = (n, pl.ds(sent, UNIT_ROWS))
        code_out[tail] = jnp.full((UNIT_ROWS, width), unit).astype(jnp.bfloat16)
        used = code_out[tail].astype(jnp.float32)[0:1]
        value = part[(n,) + cut(n % 2, 0, True)].reshape(sent, width)
        code_out[n, 0:sent] = encode(value, used)
        hop_copy(n, 0).start()

    def finish(n, hop):
        s, j = tiles[n]
        hop_copy(n, hop).wait_recv()
        index = (n,) + cut(n % 2, hop, False)
        if hop == 0:
            unit = code_in[n, sent:].astype(jnp.float32)[0:1]
            arrived = decode(code_in[n, 0:sent], unit)
            arrived = arrived.reshape((2,) * (bits - 1) + (rows, width))
        else:
            arrived = hop_refs[hop - 1][n]
        total = part[index] + arrived
        if hop < bits - 1:
            part[index] = total
            hop_copy(n, hop + 1).start()
        else:
            out_ref[s, :, j * width : (j + 1) * width] = total

    count = len(tiles)
    for n in range(count + bits):
        if n < count:
            s, j = tiles[n]
            if s > 0:
                tick = pieces.index((s - 1, j))
                ring_copy(s - 1, j).wait()
                if tick + AHEAD < len(pieces):
                    ring_copy(*pieces[tick + AHEAD]).start()
            compute(n)
        for hop in range(bits):
            if 0 <= n - 1 - hop < count:
                finish(n - 1 - hop, hop)

    for n in range(count):
        for hop in range(bits):
            hop_copy(n, hop).wait_send()


def on_device(n_aux, n_basis, factors):
    depth = factors.shape[0] * factors.shape[1]
    block = factors.shape[2]
    full = round_up(depth, 256)
    flat = jnp.transpose(factors, (1, 0, 2)).reshape(depth, block)
    bits = n_aux.bit_length() - 1
    width = 128
    chunks = block // width
    count = SHIFTS * chunks
    rows = block // n_aux
    hop_bufs = []
    for hop in range(1, bits):
        shape = (count,) + (2,) * (bits - 1 - hop) + (rows, width)
        hop_bufs.append(pltpu.VMEM(shape, jnp.float32))
    cfg = (depth, full, block, width, chunks, bits, n_aux, n_basis)
    return pl.pallas_call(
        functools.partial(kernel, cfg),
        out_shape=jax.ShapeDtypeStruct((SHIFTS, rows, block), jnp.float32),
        in_specs=[pl.BlockSpec(memory_space=pl.ANY)],
        out_specs=pl.BlockSpec(memory_space=pltpu.VMEM),
        scratch_shapes=[
            pltpu.VMEM((full, block), jnp.bfloat16),
            pltpu.VMEM((block, full), jnp.bfloat16),
            pltpu.VMEM((SHIFTS - 1, full, block), jnp.bfloat16),
            pltpu.VMEM((count,) + (2,) * bits + (rows, width), jnp.float32),
            pltpu.VMEM((count, block // 2 + UNIT_ROWS, width), jnp.bfloat16),
            pltpu.VMEM((count, block // 2 + UNIT_ROWS, width), jnp.bfloat16),
            *hop_bufs,
            pltpu.SemaphoreType.DMA((chunks,)),
            pltpu.SemaphoreType.DMA((SHIFTS - 1, chunks)),
            pltpu.SemaphoreType.DMA((SHIFTS - 1, chunks)),
            pltpu.SemaphoreType.DMA((count, bits)),
            pltpu.SemaphoreType.DMA((count, bits)),
        ],
        compiler_params=pltpu.CompilerParams(
            collective_id=0, has_side_effects=True, vmem_limit_bytes=58 * 2**20
        ),
        cost_estimate=pl.CostEstimate(
            flops=2 * SHIFTS * full * block * block,
            bytes_accessed=2 * full * block + 4 * SHIFTS * rows * block,
            transcendentals=0,
        ),
    )(flat)


def solution(mesh):
    n_aux, n_basis = mesh.shape["aux"], mesh.shape["basis"]
    return jax.shard_map(
        functools.partial(on_device, n_aux, n_basis),
        mesh=mesh,
        in_specs=(P("aux", None, "basis"),),
        out_specs=P(None, ("basis", "aux"), None),
        check_vma=False,
    )
```

```python
import functools

import jax
import jax.numpy as jnp
from jax import lax
from jax.experimental import pallas as pl
from jax.experimental.pallas import tpu as pltpu
from jax.sharding import PartitionSpec as P

SHIFTS = 3
SMALLEST = 2.0**-125
UNIT_ROWS = 16
MESH = pl.DeviceIdType.MESH


def round_up(value, step):
    return -(-value // step) * step


def encode(value, unit):
    scaled = value * (1.0 / unit)
    power = scaled * scaled
    power = power * power
    power = power * power
    return jnp.where(scaled < 0, -power, power).astype(jnp.bfloat16)


def decode(code, unit):
    code = code.astype(jnp.float32)
    fourth = lax.rsqrt(lax.rsqrt(jnp.maximum(jnp.abs(code), SMALLEST)))
    root = fourth * lax.rsqrt(fourth)
    root = jnp.where(code > 0, root, jnp.where(code < 0, -root, 0.0))
    return root * unit


def kernel(cfg, x_hbm, out_ref, x_ref, own_t, rhs, got, part, code_out, code_in, *rest):
    inner, group, full, block, width, chunks, bits, n_aux, n_basis = cfg
    depth = inner * group
    later = bits - 1
    hop_refs = rest[: 2 * later]
    load_sem, ring_send, ring_recv, hop_send, hop_recv = rest[2 * later :]
    half = width // 2
    rows = block // n_aux
    me_aux = lax.axis_index("aux")
    me_basis = lax.axis_index("basis")
    left = lax.rem(me_basis + n_basis - 1, n_basis)
    right = lax.rem(me_basis + 1, n_basis)
    my_bit = [lax.rem(me_aux // (2**q), 2) for q in range(bits)]
    partner = [me_aux + (1 - 2 * my_bit[q]) * 2**q for q in range(bits)]

    def load(j):
        here = (slice(None), slice(None), pl.ds(j * width, width))
        return pltpu.make_async_copy(x_hbm.at[here], x_ref.at[here], load_sem.at[j])

    for j in range(chunks):
        load(j).start()

    barrier = pltpu.get_barrier_semaphore()
    for who in [{"basis": left}, {"basis": right}] + [{"aux": p} for p in partner]:
        pl.semaphore_signal(barrier, inc=1, device_id=who, device_id_type=MESH)
    if full > depth:
        rhs[depth:full, :] = jnp.zeros((full - depth, width), rhs.dtype)
    pl.semaphore_wait(barrier, 2 + bits)

    def ring_copy(s, j):
        cols = pl.ds(j * width, width)
        source = x_ref if s == 0 else got.at[s - 1]
        return pltpu.make_async_remote_copy(
            src_ref=source.at[:, :, cols],
            dst_ref=got.at[s, :, :, cols],
            send_sem=ring_send.at[s, j],
            recv_sem=ring_recv.at[s, j],
            device_id={"basis": left},
            device_id_type=MESH,
        )

    def order(side):
        return list(range(bits)) if side == 0 else list(range(bits))[::-1]

    def cut(side, hop, last):
        index = [pl.ds(0, 2)] * bits
        for step, q in enumerate(order(side)[: hop + 1]):
            index[bits - 1 - q] = my_bit[q] if step < hop or not last else 1 - my_bit[q]
        return tuple(index)

    def hop_copy(n, side, hop):
        q = order(side)[hop]
        if hop == 0:
            source, target = code_out.at[n, side], code_in.at[n, side]
        else:
            source = part.at[(n, side) + cut(side, hop, True)]
            target = hop_refs[side * later + hop - 1].at[n]
        return pltpu.make_async_remote_copy(
            src_ref=source,
            dst_ref=target,
            send_sem=hop_send.at[n, side, hop],
            recv_sem=hop_recv.at[n, side, hop],
            device_id={"aux": partner[q]},
            device_id_type=MESH,
        )

    for j in range(chunks):
        load(j).wait()
        ring_copy(0, j).start()

    def flatten(s, j):
        source = x_ref if s == 0 else got.at[s - 1]
        chunk = source[:, :, j * width : (j + 1) * width]
        rhs[0:depth, :] = chunk.reshape(depth, width)

    for j in range(chunks):
        flatten(0, j)
        own_t[j * width : (j + 1) * width, :] = rhs[...].T

    tiles = [(s, j) for s in range(SHIFTS) for j in range(chunks)]
    lhs_rows = min(256, block)
    sent = block // 2

    def compute(n):
        s, j = tiles[n]
        flatten(s, j)

        def body(i, carry):
            here = pl.ds(pl.multiple_of(i * lhs_rows, lhs_rows), lhs_rows)
            product = jnp.dot(
                own_t[here, :], rhs[...], preferred_element_type=jnp.float32
            )
            per = lhs_rows // rows
            for r in range(per):
                g = i * per + r
                index = [lax.rem(g // (2**q), 2) for q in range(bits)][::-1]
                for side in range(2):
                    part[(n, side) + tuple(index)] = product[
                        r * rows : (r + 1) * rows, side * half : (side + 1) * half
                    ]
            size = jnp.abs(product).reshape(lhs_rows // 8, 8, width)
            return jnp.maximum(carry, jnp.max(size, axis=0))

        start = jnp.zeros((8, width), jnp.float32)
        most = jnp.max(lax.fori_loop(0, block // lhs_rows, body, start))
        unit = jnp.maximum(most, 2.0**-90) * 2.0**-14
        for side in range(2):
            tail = (n, side, pl.ds(sent, UNIT_ROWS))
            code_out[tail] = jnp.full((UNIT_ROWS, half), unit).astype(jnp.bfloat16)
            used = code_out[tail].astype(jnp.float32)[0:1]
            value = part[(n, side) + cut(side, 0, True)].reshape(sent, half)
            code_out[n, side, 0:sent] = encode(value, used)
            hop_copy(n, side, 0).start()

    def finish(n, hop):
        s, j = tiles[n]
        for side in range(2):
            hop_copy(n, side, hop).wait_recv()
            index = (n, side) + cut(side, hop, False)
            if hop == 0:
                unit = code_in[n, side, sent:].astype(jnp.float32)[0:1]
                arrived = decode(code_in[n, side, 0:sent], unit)
                arrived = arrived.reshape((2,) * (bits - 1) + (rows, half))
            else:
                arrived = hop_refs[side * later + hop - 1][n]
            total = part[index] + arrived
            if hop < bits - 1:
                part[index] = total
                hop_copy(n, side, hop + 1).start()
            else:
                out_ref[s, :, j * width + side * half : j * width + (side + 1) * half] = total

    count = len(tiles)
    done = {}

    def catch_up(last, lag):
        for hop in range(bits):
            for m in range(done.get(hop, 0), max(last - lag * hop + 1, 0)):
                finish(m, hop)
                done[hop] = m + 1

    for n in range(count):
        s, j = tiles[n]
        if s > 0:
            if s == SHIFTS - 1:
                catch_up(n - 1, 0)
            ring_copy(s - 1, j).wait_recv()
            if s < SHIFTS - 1:
                ring_copy(s, j).start()
        compute(n)
        catch_up(n - 1, 1)
    catch_up(count - 1, 0)

    for s in range(SHIFTS - 1):
        for j in range(chunks):
            ring_copy(s, j).wait_send()
    for n in range(count):
        for side in range(2):
            for hop in range(bits):
                hop_copy(n, side, hop).wait_send()


def on_device(n_aux, n_basis, factors):
    group, inner = factors.shape[0], factors.shape[1]
    depth = inner * group
    block = factors.shape[2]
    full = round_up(depth, 256)
    flat = jnp.transpose(factors, (1, 0, 2))
    bits = n_aux.bit_length() - 1
    width = 256
    chunks = block // width
    count = SHIFTS * chunks
    rows = block // n_aux
    half = width // 2
    hop_bufs = []
    for side in range(2):
        for hop in range(1, bits):
            shape = (count,) + (2,) * (bits - 1 - hop) + (rows, half)
            hop_bufs.append(pltpu.VMEM(shape, jnp.float32))
    cfg = (inner, group, full, block, width, chunks, bits, n_aux, n_basis)
    return pl.pallas_call(
        functools.partial(kernel, cfg),
        out_shape=jax.ShapeDtypeStruct((SHIFTS, rows, block), jnp.float32),
        in_specs=[pl.BlockSpec(memory_space=pl.ANY)],
        out_specs=pl.BlockSpec(memory_space=pltpu.VMEM),
        scratch_shapes=[
            pltpu.VMEM((inner, group, block), jnp.bfloat16),
            pltpu.VMEM((block, full), jnp.bfloat16),
            pltpu.VMEM((full, width), jnp.bfloat16),
            pltpu.VMEM((SHIFTS - 1, inner, group, block), jnp.bfloat16),
            pltpu.VMEM((count, 2) + (2,) * bits + (rows, half), jnp.float32),
            pltpu.VMEM((count, 2, block // 2 + UNIT_ROWS, half), jnp.bfloat16),
            pltpu.VMEM((count, 2, block // 2 + UNIT_ROWS, half), jnp.bfloat16),
            *hop_bufs,
            pltpu.SemaphoreType.DMA((chunks,)),
            pltpu.SemaphoreType.DMA((SHIFTS - 1, chunks)),
            pltpu.SemaphoreType.DMA((SHIFTS - 1, chunks)),
            pltpu.SemaphoreType.DMA((count, 2, bits)),
            pltpu.SemaphoreType.DMA((count, 2, bits)),
        ],
        compiler_params=pltpu.CompilerParams(
            collective_id=0, has_side_effects=True, vmem_limit_bytes=58 * 2**20
        ),
        cost_estimate=pl.CostEstimate(
            flops=2 * SHIFTS * full * block * block,
            bytes_accessed=2 * full * block + 4 * SHIFTS * rows * block,
            transcendentals=0,
        ),
    )(flat)


def solution(mesh):
    n_aux, n_basis = mesh.shape["aux"], mesh.shape["basis"]
    return jax.shard_map(
        functools.partial(on_device, n_aux, n_basis),
        mesh=mesh,
        in_specs=(P("aux", None, "basis"),),
        out_specs=P(None, ("basis", "aux"), None),
        check_vma=False,
    )
```

```python
import functools

import jax
import jax.numpy as jnp
from jax import lax
from jax.experimental import pallas as pl
from jax.experimental.pallas import tpu as pltpu
from jax.sharding import PartitionSpec as P

SHIFTS = 3
SMALLEST = 2.0**-125
UNIT_ROWS = 16
MESH = pl.DeviceIdType.MESH


def round_up(value, step):
    return -(-value // step) * step


def encode(value, unit):
    scaled = value * (1.0 / unit)
    power = scaled * scaled
    power = power * power
    power = power * power
    return jnp.where(scaled < 0, -power, power).astype(jnp.bfloat16)


def decode(code, unit):
    code = code.astype(jnp.float32)
    fourth = lax.rsqrt(lax.rsqrt(jnp.maximum(jnp.abs(code), SMALLEST)))
    root = fourth * lax.rsqrt(fourth)
    root = jnp.where(code > 0, root, jnp.where(code < 0, -root, 0.0))
    return root * unit


def kernel(cfg, x_hbm, out_hbm, x_ref, out_ref, own_t, rhs, got, part, code_out, code_in, *rest):
    inner, group, full, block, width, chunks, bits, n_aux, n_basis = cfg
    depth = inner * group
    later = bits - 1
    hop_refs = rest[: 2 * later]
    load_sem, store_sem, ring_send, ring_recv, hop_send, hop_recv = rest[2 * later :]
    half = width // 2
    rows = block // n_aux
    me_aux = lax.axis_index("aux")
    me_basis = lax.axis_index("basis")
    left = lax.rem(me_basis + n_basis - 1, n_basis)
    right = lax.rem(me_basis + 1, n_basis)
    my_bit = [lax.rem(me_aux // (2**q), 2) for q in range(bits)]
    partner = [me_aux + (1 - 2 * my_bit[q]) * 2**q for q in range(bits)]

    def load(j):
        here = (slice(None), slice(None), pl.ds(j * width, width))
        return pltpu.make_async_copy(x_hbm.at[here], x_ref.at[here], load_sem.at[j])

    for j in range(chunks):
        load(j).start()

    barrier = pltpu.get_barrier_semaphore()
    for who in [{"basis": left}, {"basis": right}] + [{"aux": p} for p in partner]:
        pl.semaphore_signal(barrier, inc=1, device_id=who, device_id_type=MESH)
    if full > depth:
        rhs[depth:full, :] = jnp.zeros((full - depth, width), rhs.dtype)
    pl.semaphore_wait(barrier, 2 + bits)

    def ring_copy(s, j, low=0, high=inner):
        cols = pl.ds(j * width, width)
        source = x_ref if s == 0 else got.at[s - 1]
        return pltpu.make_async_remote_copy(
            src_ref=source.at[pl.ds(low, high - low), :, cols],
            dst_ref=got.at[s, pl.ds(low, high - low), :, cols],
            send_sem=ring_send.at[s, j if low == 0 else chunks],
            recv_sem=ring_recv.at[s, j if low == 0 else chunks],
            device_id={"basis": left},
            device_id_type=MESH,
        )

    def order(side):
        return list(range(bits)) if side == 0 else list(range(bits))[::-1]

    def cut(side, hop, last):
        index = [pl.ds(0, 2)] * bits
        for step, q in enumerate(order(side)[: hop + 1]):
            index[bits - 1 - q] = my_bit[q] if step < hop or not last else 1 - my_bit[q]
        return tuple(index)

    def hop_copy(n, side, hop):
        q = order(side)[hop]
        if hop == 0:
            source, target = code_out.at[n, side], code_in.at[n, side]
        else:
            source = part.at[(n, side) + cut(side, hop, True)]
            target = hop_refs[side * later + hop - 1].at[n]
        return pltpu.make_async_remote_copy(
            src_ref=source,
            dst_ref=target,
            send_sem=hop_send.at[n, side, hop],
            recv_sem=hop_recv.at[n, side, hop],
            device_id={"aux": partner[q]},
            device_id_type=MESH,
        )

    for j in range(chunks):
        load(j).wait()
        ring_copy(0, j).start()

    def flatten(s, j, low=0, high=inner):
        source = x_ref if s == 0 else got.at[s - 1]
        chunk = source[low:high, :, j * width : (j + 1) * width]
        chunk = chunk.reshape((high - low) * group, width)
        rhs[low * group : high * group, :] = chunk

    for j in range(chunks):
        flatten(0, j)
        own_t[j * width : (j + 1) * width, :] = rhs[...].T

    tiles = [(s, j) for s in range(SHIFTS) for j in range(chunks)]
    lhs_rows = min(256, block)
    sent = block // 2
    middle = round_up(depth * 3 // 4, 256) // group

    def multiply(n, low, high, add):
        def body(i, most):
            here = pl.ds(pl.multiple_of(i * lhs_rows, lhs_rows), lhs_rows)
            product = jnp.dot(
                own_t[here, low:high],
                rhs[low:high, :],
                preferred_element_type=jnp.float32,
            )
            per = lhs_rows // rows
            for r in range(per):
                g = i * per + r
                index = [lax.rem(g // (2**q), 2) for q in range(bits)][::-1]
                for side in range(2):
                    place = (n, side) + tuple(index)
                    value = product[
                        r * rows : (r + 1) * rows, side * half : (side + 1) * half
                    ]
                    if add:
                        value = value + part[place]
                    part[place] = value
                    size = jnp.abs(value).reshape(rows // 8, 8, half)
                    most = jnp.maximum(most, jnp.max(size, axis=0))
            return most

        start = jnp.zeros((8, half), jnp.float32)
        return lax.fori_loop(0, block // lhs_rows, body, start)

    def send_first(n, most):
        most = jnp.max(most)
        unit = jnp.maximum(most, 2.0**-90) * 2.0**-14
        for side in range(2):
            tail = (n, side, pl.ds(sent, UNIT_ROWS))
            code_out[tail] = jnp.full((UNIT_ROWS, half), unit).astype(jnp.bfloat16)
            used = code_out[tail].astype(jnp.float32)[0:1]
            value = part[(n, side) + cut(side, 0, True)].reshape(sent, half)
            code_out[n, side, 0:sent] = encode(value, used)
            hop_copy(n, side, 0).start()

    def store(n):
        s, j = tiles[n]
        here = (s, slice(None), pl.ds(j * width, width))
        return pltpu.make_async_copy(out_ref.at[here], out_hbm.at[here], store_sem.at[n])

    def finish(n, hop):
        s, j = tiles[n]
        for side in range(2):
            hop_copy(n, side, hop).wait_recv()
            index = (n, side) + cut(side, hop, False)
            if hop == 0:
                unit = code_in[n, side, sent:].astype(jnp.float32)[0:1]
                arrived = decode(code_in[n, side, 0:sent], unit)
                arrived = arrived.reshape((2,) * (bits - 1) + (rows, half))
            else:
                arrived = hop_refs[side * later + hop - 1][n]
            total = part[index] + arrived
            if hop < bits - 1:
                part[index] = total
                hop_copy(n, side, hop + 1).start()
            else:
                out_ref[s, :, j * width + side * half : j * width + (side + 1) * half] = total
        if hop == bits - 1:
            store(n).start()

    count = len(tiles)
    done = {}

    def catch_up(last, lag):
        for hop in range(bits):
            for m in range(done.get(hop, 0), max(last - lag * hop + 1, 0)):
                finish(m, hop)
                done[hop] = m + 1

    for n in range(count):
        s, j = tiles[n]
        split = n == count - 1
        if s > 0:
            if s == SHIFTS - 1:
                catch_up(n - 1, 0)
            ring_copy(s - 1, j, 0, middle if split else inner).wait_recv()
            if s == SHIFTS - 2 and j == chunks - 1:
                ring_copy(s, j, 0, middle).start()
                ring_copy(s, j, middle, inner).start()
            elif s < SHIFTS - 1:
                ring_copy(s, j).start()
        if split:
            flatten(s, j, 0, middle)
            multiply(n, 0, middle * group, False)
            ring_copy(s - 1, j, middle, inner).wait_recv()
            flatten(s, j, middle, inner)
            send_first(n, multiply(n, middle * group, full, True))
        else:
            flatten(s, j)
            send_first(n, multiply(n, 0, full, False))
        catch_up(n - 1, 1)
    catch_up(count - 1, 0)

    for s in range(SHIFTS - 1):
        for j in range(chunks):
            if (s, j) == (SHIFTS - 2, chunks - 1):
                ring_copy(s, j, 0, middle).wait_send()
                ring_copy(s, j, middle, inner).wait_send()
            else:
                ring_copy(s, j).wait_send()
    for n in range(count):
        store(n).wait()
    for n in range(count):
        for side in range(2):
            for hop in range(bits):
                hop_copy(n, side, hop).wait_send()


def on_device(n_aux, n_basis, factors):
    group, inner = factors.shape[0], factors.shape[1]
    depth = inner * group
    block = factors.shape[2]
    full = round_up(depth, 256)
    flat = jnp.transpose(factors, (1, 0, 2))
    bits = n_aux.bit_length() - 1
    width = 256
    chunks = block // width
    count = SHIFTS * chunks
    rows = block // n_aux
    half = width // 2
    hop_bufs = []
    for side in range(2):
        for hop in range(1, bits):
            shape = (count,) + (2,) * (bits - 1 - hop) + (rows, half)
            hop_bufs.append(pltpu.VMEM(shape, jnp.float32))
    cfg = (inner, group, full, block, width, chunks, bits, n_aux, n_basis)
    return pl.pallas_call(
        functools.partial(kernel, cfg),
        out_shape=jax.ShapeDtypeStruct((SHIFTS, rows, block), jnp.float32),
        in_specs=[pl.BlockSpec(memory_space=pl.ANY)],
        out_specs=pl.BlockSpec(memory_space=pl.ANY),
        scratch_shapes=[
            pltpu.VMEM((inner, group, block), jnp.bfloat16),
            pltpu.VMEM((SHIFTS, rows, block), jnp.float32),
            pltpu.VMEM((block, full), jnp.bfloat16),
            pltpu.VMEM((full, width), jnp.bfloat16),
            pltpu.VMEM((SHIFTS - 1, inner, group, block), jnp.bfloat16),
            pltpu.VMEM((count, 2) + (2,) * bits + (rows, half), jnp.float32),
            pltpu.VMEM((count, 2, block // 2 + UNIT_ROWS, half), jnp.bfloat16),
            pltpu.VMEM((count, 2, block // 2 + UNIT_ROWS, half), jnp.bfloat16),
            *hop_bufs,
            pltpu.SemaphoreType.DMA((chunks,)),
            pltpu.SemaphoreType.DMA((count,)),
            pltpu.SemaphoreType.DMA((SHIFTS - 1, chunks + 1)),
            pltpu.SemaphoreType.DMA((SHIFTS - 1, chunks + 1)),
            pltpu.SemaphoreType.DMA((count, 2, bits)),
            pltpu.SemaphoreType.DMA((count, 2, bits)),
        ],
        compiler_params=pltpu.CompilerParams(
            collective_id=0, has_side_effects=True, vmem_limit_bytes=58 * 2**20
        ),
        cost_estimate=pl.CostEstimate(
            flops=2 * SHIFTS * full * block * block,
            bytes_accessed=2 * full * block + 4 * SHIFTS * rows * block,
            transcendentals=0,
        ),
    )(flat)


def solution(mesh):
    n_aux, n_basis = mesh.shape["aux"], mesh.shape["basis"]
    return jax.shard_map(
        functools.partial(on_device, n_aux, n_basis),
        mesh=mesh,
        in_specs=(P("aux", None, "basis"),),
        out_specs=P(None, ("basis", "aux"), None),
        check_vma=False,
    )
```

```python
import functools

import jax
import jax.numpy as jnp
from jax import lax
from jax.experimental import pallas as pl
from jax.experimental.pallas import tpu as pltpu
from jax.sharding import PartitionSpec as P

SHIFTS = 3
SMALLEST = 2.0**-125
UNIT_ROWS = 16
MESH = pl.DeviceIdType.MESH


def round_up(value, step):
    return -(-value // step) * step


def encode(value, unit):
    scaled = value * (1.0 / unit)
    power = scaled * scaled
    power = power * power
    power = power * power
    return jnp.where(scaled < 0, -power, power).astype(jnp.bfloat16)


def decode(code, unit):
    code = code.astype(jnp.float32)
    fourth = lax.rsqrt(lax.rsqrt(jnp.maximum(jnp.abs(code), SMALLEST)))
    root = fourth * lax.rsqrt(fourth)
    root = jnp.where(code > 0, root, jnp.where(code < 0, -root, 0.0))
    return root * unit


def kernel(cfg, x_hbm, out_hbm, x_ref, out_ref, own_t, rhs, got, part, code_out, code_in, *rest):
    inner, group, full, block, width, chunks, bits, n_aux, n_basis = cfg
    depth = inner * group
    later = bits - 1
    hop_refs = rest[: 2 * later]
    load_sem, store_sem, ring_send, ring_recv, hop_send, hop_recv = rest[2 * later :]
    half = width // 2
    rows = block // n_aux
    me_aux = lax.axis_index("aux")
    me_basis = lax.axis_index("basis")
    left = lax.rem(me_basis + n_basis - 1, n_basis)
    right = lax.rem(me_basis + 1, n_basis)
    my_bit = [lax.rem(me_aux // (2**q), 2) for q in range(bits)]
    partner = [me_aux + (1 - 2 * my_bit[q]) * 2**q for q in range(bits)]

    def load(j):
        here = (slice(None), slice(None), pl.ds(j * width, width))
        return pltpu.make_async_copy(x_hbm.at[here], x_ref.at[here], load_sem.at[j])

    for j in range(chunks):
        load(j).start()

    barrier = pltpu.get_barrier_semaphore()
    for who in [{"basis": left}, {"basis": right}] + [{"aux": p} for p in partner]:
        pl.semaphore_signal(barrier, inc=1, device_id=who, device_id_type=MESH)
    if full > depth:
        rhs[depth:full, :] = jnp.zeros((full - depth, width), rhs.dtype)
    pl.semaphore_wait(barrier, 2 + bits)

    def ring_copy(s, j, low=0, high=inner):
        cols = pl.ds(j * width, width)
        source = x_ref if s == 0 else got.at[s - 1]
        return pltpu.make_async_remote_copy(
            src_ref=source.at[pl.ds(low, high - low), :, cols],
            dst_ref=got.at[s, pl.ds(low, high - low), :, cols],
            send_sem=ring_send.at[s, j if low == 0 else chunks],
            recv_sem=ring_recv.at[s, j if low == 0 else chunks],
            device_id={"basis": left},
            device_id_type=MESH,
        )

    def order(side):
        return list(range(bits)) if side == 0 else list(range(bits))[::-1]

    def cut(side, hop, last):
        index = [pl.ds(0, 2)] * bits
        for step, q in enumerate(order(side)[: hop + 1]):
            index[bits - 1 - q] = my_bit[q] if step < hop or not last else 1 - my_bit[q]
        return tuple(index)

    def hop_copy(n, side, hop):
        q = order(side)[hop]
        if hop == 0:
            source, target = code_out.at[n, side], code_in.at[n, side]
        else:
            source = part.at[(n, side) + cut(side, hop, True)]
            target = hop_refs[side * later + hop - 1].at[n]
        return pltpu.make_async_remote_copy(
            src_ref=source,
            dst_ref=target,
            send_sem=hop_send.at[n, side, hop],
            recv_sem=hop_recv.at[n, side, hop],
            device_id={"aux": partner[q]},
            device_id_type=MESH,
        )

    for j in range(chunks):
        load(j).wait()
        ring_copy(0, j).start()

    def flatten(s, j, low=0, high=inner):
        source = x_ref if s == 0 else got.at[s - 1]
        chunk = source[low:high, :, j * width : (j + 1) * width]
        chunk = chunk.reshape((high - low) * group, width)
        rhs[low * group : high * group, :] = chunk

    for j in range(chunks):
        flatten(0, j)
        own_t[j * width : (j + 1) * width, :] = rhs[...].T

    tiles = [(s, j) for s in range(SHIFTS) for j in range(chunks)]
    lhs_rows = min(256, block)
    sent = block // 2
    middle = round_up(depth * 3 // 4, 256) // group

    def multiply(n, low, high, add):
        def body(i, most):
            here = pl.ds(pl.multiple_of(i * lhs_rows, lhs_rows), lhs_rows)
            product = jnp.dot(
                own_t[here, low:high],
                rhs[low:high, :],
                preferred_element_type=jnp.float32,
            )
            per = lhs_rows // rows
            for r in range(per):
                g = i * per + r
                index = [lax.rem(g // (2**q), 2) for q in range(bits)][::-1]
                for side in range(2):
                    place = (n, side) + tuple(index)
                    value = product[
                        r * rows : (r + 1) * rows, side * half : (side + 1) * half
                    ]
                    if add:
                        value = value + part[place]
                    part[place] = value
                    size = jnp.abs(value).reshape(rows // 8, 8, half)
                    most = jnp.maximum(most, jnp.max(size, axis=0))
            return most

        start = jnp.zeros((8, half), jnp.float32)
        return lax.fori_loop(0, block // lhs_rows, body, start)

    def send_first(n, most):
        most = jnp.max(most)
        unit = jnp.maximum(most, 2.0**-90) * 2.0**-14
        for side in range(2):
            tail = (n, side, pl.ds(sent, UNIT_ROWS))
            code_out[tail] = jnp.full((UNIT_ROWS, half), unit).astype(jnp.bfloat16)
            used = code_out[tail].astype(jnp.float32)[0:1]
            value = part[(n, side) + cut(side, 0, True)].reshape(sent, half)
            code_out[n, side, 0:sent] = encode(value, used)
            hop_copy(n, side, 0).start()

    def store(n):
        s, j = tiles[n]
        here = (s, slice(None), pl.ds(j * width, width))
        return pltpu.make_async_copy(out_ref.at[here], out_hbm.at[here], store_sem.at[n])

    def finish(n, hop):
        s, j = tiles[n]
        for side in range(2):
            hop_copy(n, side, hop).wait_recv()
            index = (n, side) + cut(side, hop, False)
            if hop == 0:
                unit = code_in[n, side, sent:].astype(jnp.float32)[0:1]
                arrived = decode(code_in[n, side, 0:sent], unit)
                arrived = arrived.reshape((2,) * (bits - 1) + (rows, half))
            else:
                arrived = hop_refs[side * later + hop - 1][n]
            total = part[index] + arrived
            if hop < bits - 1:
                part[index] = total
                hop_copy(n, side, hop + 1).start()
            else:
                out_ref[s, :, j * width + side * half : j * width + (side + 1) * half] = total
        if hop == bits - 1:
            store(n).start()

    count = len(tiles)
    done = {}

    def catch_up(last, lag):
        for hop in range(bits):
            for m in range(done.get(hop, 0), max(last - lag * hop + 1, 0)):
                finish(m, hop)
                done[hop] = m + 1

    for n in range(count):
        s, j = tiles[n]
        split = n == count - 1
        if s > 0:
            if s == SHIFTS - 1:
                catch_up(n - 1, 0)
            ring_copy(s - 1, j, 0, middle if split else inner).wait_recv()
            if s == SHIFTS - 2 and j == chunks - 1:
                ring_copy(s, j, 0, middle).start()
                ring_copy(s, j, middle, inner).start()
            elif s < SHIFTS - 1:
                ring_copy(s, j).start()
        if split:
            flatten(s, j, 0, middle)
            multiply(n, 0, middle * group, False)
            ring_copy(s - 1, j, middle, inner).wait_recv()
            flatten(s, j, middle, inner)
            send_first(n, multiply(n, middle * group, full, True))
        else:
            flatten(s, j)
            send_first(n, multiply(n, 0, full, False))
        catch_up(n - 1, 1)
    catch_up(count - 1, 0)

    for s in range(SHIFTS - 1):
        for j in range(chunks):
            if (s, j) == (SHIFTS - 2, chunks - 1):
                ring_copy(s, j, 0, middle).wait_send()
                ring_copy(s, j, middle, inner).wait_send()
            else:
                ring_copy(s, j).wait_send()
    for n in range(count):
        store(n).wait()
    for n in range(count):
        for side in range(2):
            for hop in range(bits):
                hop_copy(n, side, hop).wait_send()


def hand_on(parts, source, target, sems):
    per = source.shape[1] // parts
    copies = []
    for s in range(SHIFTS):
        for i in range(parts):
            here = (s, pl.ds(i * per, per))
            sem = sems.at[s * parts + i]
            copies.append(pltpu.make_async_copy(source.at[here], target.at[here], sem))
    for copy in copies:
        copy.start()
    for copy in copies:
        copy.wait()


def on_device(n_aux, n_basis, factors):
    group, inner = factors.shape[0], factors.shape[1]
    depth = inner * group
    block = factors.shape[2]
    full = round_up(depth, 256)
    flat = jnp.transpose(factors, (1, 0, 2))
    bits = n_aux.bit_length() - 1
    width = 256
    chunks = block // width
    count = SHIFTS * chunks
    rows = block // n_aux
    half = width // 2
    hop_bufs = []
    for side in range(2):
        for hop in range(1, bits):
            shape = (count,) + (2,) * (bits - 1 - hop) + (rows, half)
            hop_bufs.append(pltpu.VMEM(shape, jnp.float32))
    cfg = (inner, group, full, block, width, chunks, bits, n_aux, n_basis)
    result = pl.pallas_call(
        functools.partial(kernel, cfg),
        out_shape=jax.ShapeDtypeStruct((SHIFTS, rows, block), jnp.float32),
        in_specs=[pl.BlockSpec(memory_space=pl.ANY)],
        out_specs=pl.BlockSpec(memory_space=pl.ANY),
        scratch_shapes=[
            pltpu.VMEM((inner, group, block), jnp.bfloat16),
            pltpu.VMEM((SHIFTS, rows, block), jnp.float32),
            pltpu.VMEM((block, full), jnp.bfloat16),
            pltpu.VMEM((full, width), jnp.bfloat16),
            pltpu.VMEM((SHIFTS - 1, inner, group, block), jnp.bfloat16),
            pltpu.VMEM((count, 2) + (2,) * bits + (rows, half), jnp.float32),
            pltpu.VMEM((count, 2, block // 2 + UNIT_ROWS, half), jnp.bfloat16),
            pltpu.VMEM((count, 2, block // 2 + UNIT_ROWS, half), jnp.bfloat16),
            *hop_bufs,
            pltpu.SemaphoreType.DMA((chunks,)),
            pltpu.SemaphoreType.DMA((count,)),
            pltpu.SemaphoreType.DMA((SHIFTS - 1, chunks + 1)),
            pltpu.SemaphoreType.DMA((SHIFTS - 1, chunks + 1)),
            pltpu.SemaphoreType.DMA((count, 2, bits)),
            pltpu.SemaphoreType.DMA((count, 2, bits)),
        ],
        compiler_params=pltpu.CompilerParams(
            collective_id=0, has_side_effects=True, vmem_limit_bytes=58 * 2**20
        ),
        cost_estimate=pl.CostEstimate(
            flops=2 * SHIFTS * full * block * block,
            bytes_accessed=2 * full * block + 4 * SHIFTS * rows * block,
            transcendentals=0,
        ),
    )(flat)
    parts = 4 if rows % 32 == 0 else 1
    return pl.pallas_call(
        functools.partial(hand_on, parts),
        out_shape=jax.ShapeDtypeStruct(result.shape, result.dtype),
        in_specs=[pl.BlockSpec(memory_space=pl.ANY)],
        out_specs=pl.BlockSpec(memory_space=pl.ANY),
        scratch_shapes=[pltpu.SemaphoreType.DMA((SHIFTS * parts,))],
        cost_estimate=pl.CostEstimate(
            flops=0, bytes_accessed=8 * SHIFTS * rows * block, transcendentals=0
        ),
    )(result)


def solution(mesh):
    n_aux, n_basis = mesh.shape["aux"], mesh.shape["basis"]
    return jax.shard_map(
        functools.partial(on_device, n_aux, n_basis),
        mesh=mesh,
        in_specs=(P("aux", None, "basis"),),
        out_specs=P(None, ("basis", "aux"), None),
        check_vma=False,
    )
```

```python
import functools

import jax
import jax.numpy as jnp
from jax import lax
from jax.experimental import pallas as pl
from jax.experimental.pallas import tpu as pltpu
from jax.sharding import PartitionSpec as P

SHIFTS = 3
SMALLEST = 2.0**-125
UNIT_ROWS = 16
MESH = pl.DeviceIdType.MESH


def round_up(value, step):
    return -(-value // step) * step


def encode(value, unit):
    scaled = value * (1.0 / unit)
    power = scaled * scaled
    power = power * power
    power = power * power
    return jnp.where(scaled < 0, -power, power).astype(jnp.bfloat16)


def decode(code, unit):
    code = code.astype(jnp.float32)
    fourth = lax.rsqrt(lax.rsqrt(jnp.maximum(jnp.abs(code), SMALLEST)))
    root = fourth * lax.rsqrt(fourth)
    root = jnp.where(code > 0, root, jnp.where(code < 0, -root, 0.0))
    return root * unit


def kernel(cfg, x_hbm, out_hbm, x_ref, out_ref, own_t, rhs, got, part, code_out, code_in, *rest):
    inner, group, full, block, width, chunks, bits, n_aux, n_basis = cfg
    depth = inner * group
    later = bits - 1
    hop_refs = rest[: 2 * later]
    load_sem, store_sem, ring_send, ring_recv, hop_send, hop_recv = rest[2 * later :]
    half = width // 2
    rows = block // n_aux
    me_aux = lax.axis_index("aux")
    me_basis = lax.axis_index("basis")
    left = lax.rem(me_basis + n_basis - 1, n_basis)
    right = lax.rem(me_basis + 1, n_basis)
    my_bit = [lax.rem(me_aux // (2**q), 2) for q in range(bits)]
    partner = [me_aux + (1 - 2 * my_bit[q]) * 2**q for q in range(bits)]

    def load(j):
        here = (slice(None), slice(None), pl.ds(j * width, width))
        return pltpu.make_async_copy(x_hbm.at[here], x_ref.at[here], load_sem.at[j])

    for j in range(chunks):
        load(j).start()

    barrier = pltpu.get_barrier_semaphore()
    for who in [{"basis": left}, {"basis": right}] + [{"aux": p} for p in partner]:
        pl.semaphore_signal(barrier, inc=1, device_id=who, device_id_type=MESH)
    if full > depth:
        rhs[depth:full, :] = jnp.zeros((full - depth, width), rhs.dtype)
    pl.semaphore_wait(barrier, 2 + bits)

    def ring_copy(s, j, low=0, high=inner):
        cols = pl.ds(j * width, width)
        source = x_ref if s == 0 else got.at[s - 1]
        return pltpu.make_async_remote_copy(
            src_ref=source.at[pl.ds(low, high - low), :, cols],
            dst_ref=got.at[s, pl.ds(low, high - low), :, cols],
            send_sem=ring_send.at[s, j if low == 0 else chunks],
            recv_sem=ring_recv.at[s, j if low == 0 else chunks],
            device_id={"basis": left},
            device_id_type=MESH,
        )

    def order(side):
        return list(range(bits)) if side == 0 else list(range(bits))[::-1]

    def cut(side, hop, last):
        index = [pl.ds(0, 2)] * bits
        for step, q in enumerate(order(side)[: hop + 1]):
            index[bits - 1 - q] = my_bit[q] if step < hop or not last else 1 - my_bit[q]
        return tuple(index)

    def hop_copy(n, side, hop):
        q = order(side)[hop]
        if hop == 0:
            source, target = code_out.at[n, side], code_in.at[n, side]
        else:
            source = part.at[(n, side) + cut(side, hop, True)]
            target = hop_refs[side * later + hop - 1].at[n]
        return pltpu.make_async_remote_copy(
            src_ref=source,
            dst_ref=target,
            send_sem=hop_send.at[n, side, hop],
            recv_sem=hop_recv.at[n, side, hop],
            device_id={"aux": partner[q]},
            device_id_type=MESH,
        )

    for j in range(chunks):
        load(j).wait()
        ring_copy(0, j).start()

    def flatten(s, j, low=0, high=inner):
        source = x_ref if s == 0 else got.at[s - 1]
        chunk = source[low:high, :, j * width : (j + 1) * width]
        chunk = chunk.reshape((high - low) * group, width)
        rhs[low * group : high * group, :] = chunk

    for j in range(chunks):
        flatten(0, j)
        own_t[j * width : (j + 1) * width, :] = rhs[...].T

    tiles = [(s, j) for s in range(SHIFTS) for j in range(chunks)]
    lhs_rows = min(256, block)
    sent = block // 2
    middle = round_up(depth * 3 // 4, 256) // group

    def multiply(n, low, high, add):
        def body(i, most):
            here = pl.ds(pl.multiple_of(i * lhs_rows, lhs_rows), lhs_rows)
            product = jnp.dot(
                own_t[here, low:high],
                rhs[low:high, :],
                preferred_element_type=jnp.float32,
            )
            per = lhs_rows // rows
            for r in range(per):
                g = i * per + r
                index = [lax.rem(g // (2**q), 2) for q in range(bits)][::-1]
                for side in range(2):
                    place = (n, side) + tuple(index)
                    value = product[
                        r * rows : (r + 1) * rows, side * half : (side + 1) * half
                    ]
                    if add:
                        value = value + part[place]
                    part[place] = value
                    size = jnp.abs(value).reshape(rows // 8, 8, half)
                    most = jnp.maximum(most, jnp.max(size, axis=0))
            return most

        start = jnp.zeros((8, half), jnp.float32)
        return lax.fori_loop(0, block // lhs_rows, body, start)

    def send_first(n, most):
        most = jnp.max(most)
        unit = jnp.maximum(most, 2.0**-90) * 2.0**-14
        for side in range(2):
            tail = (n, side, pl.ds(sent, UNIT_ROWS))
            code_out[tail] = jnp.full((UNIT_ROWS, half), unit).astype(jnp.bfloat16)
            used = code_out[tail].astype(jnp.float32)[0:1]
            value = part[(n, side) + cut(side, 0, True)].reshape(sent, half)
            code_out[n, side, 0:sent] = encode(value, used)
            hop_copy(n, side, 0).start()

    def store(n):
        s, j = tiles[n]
        here = (s, slice(None), pl.ds(j * width, width))
        return pltpu.make_async_copy(out_ref.at[here], out_hbm.at[here], store_sem.at[n])

    def finish(n, hop):
        s, j = tiles[n]
        for side in range(2):
            hop_copy(n, side, hop).wait_recv()
            index = (n, side) + cut(side, hop, False)
            if hop == 0:
                unit = code_in[n, side, sent:].astype(jnp.float32)[0:1]
                arrived = decode(code_in[n, side, 0:sent], unit)
                arrived = arrived.reshape((2,) * (bits - 1) + (rows, half))
            else:
                arrived = hop_refs[side * later + hop - 1][n]
            total = part[index] + arrived
            if hop < bits - 1:
                part[index] = total
                hop_copy(n, side, hop + 1).start()
            else:
                out_ref[s, :, j * width + side * half : j * width + (side + 1) * half] = total
        if hop == bits - 1:
            store(n).start()

    count = len(tiles)
    done = {}

    def catch_up(last, lag):
        for hop in range(bits):
            for m in range(done.get(hop, 0), max(last - lag * hop + 1, 0)):
                finish(m, hop)
                done[hop] = m + 1

    for n in range(count):
        s, j = tiles[n]
        split = n == count - 1
        if s > 0:
            if s == SHIFTS - 1:
                catch_up(n - 1, 0)
            ring_copy(s - 1, j, 0, middle if split else inner).wait_recv()
            if s == SHIFTS - 2 and j == chunks - 1:
                ring_copy(s, j, 0, middle).start()
                ring_copy(s, j, middle, inner).start()
            elif s < SHIFTS - 1:
                ring_copy(s, j).start()
        if split:
            flatten(s, j, 0, middle)
            multiply(n, 0, middle * group, False)
            ring_copy(s - 1, j, middle, inner).wait_recv()
            flatten(s, j, middle, inner)
            send_first(n, multiply(n, middle * group, full, True))
        else:
            flatten(s, j)
            send_first(n, multiply(n, 0, full, False))
        catch_up(n - 1, 1)
    catch_up(count - 1, 0)

    for s in range(SHIFTS - 1):
        for j in range(chunks):
            if (s, j) == (SHIFTS - 2, chunks - 1):
                ring_copy(s, j, 0, middle).wait_send()
                ring_copy(s, j, middle, inner).wait_send()
            else:
                ring_copy(s, j).wait_send()
    for n in range(count):
        store(n).wait()
    for n in range(count):
        for side in range(2):
            for hop in range(bits):
                hop_copy(n, side, hop).wait_send()


def hand_on(parts, source, target, held, sems):
    per = source.shape[1] // parts
    pairs = []
    for s in range(SHIFTS):
        for i in range(parts):
            here, k = (s, pl.ds(i * per, per)), s * parts + i
            into = pltpu.make_async_copy(source.at[here], held.at[here], sems.at[0, k])
            out = pltpu.make_async_copy(held.at[here], target.at[here], sems.at[1, k])
            pairs.append((into, out))
    for into, _ in pairs:
        into.start()
    for into, out in pairs:
        into.wait()
        out.start()
    for _, out in pairs:
        out.wait()


def on_device(n_aux, n_basis, factors):
    group, inner = factors.shape[0], factors.shape[1]
    depth = inner * group
    block = factors.shape[2]
    full = round_up(depth, 256)
    flat = jnp.transpose(factors, (1, 0, 2))
    bits = n_aux.bit_length() - 1
    width = 256
    chunks = block // width
    count = SHIFTS * chunks
    rows = block // n_aux
    half = width // 2
    hop_bufs = []
    for side in range(2):
        for hop in range(1, bits):
            shape = (count,) + (2,) * (bits - 1 - hop) + (rows, half)
            hop_bufs.append(pltpu.VMEM(shape, jnp.float32))
    cfg = (inner, group, full, block, width, chunks, bits, n_aux, n_basis)
    result = pl.pallas_call(
        functools.partial(kernel, cfg),
        out_shape=jax.ShapeDtypeStruct((SHIFTS, rows, block), jnp.float32),
        in_specs=[pl.BlockSpec(memory_space=pl.ANY)],
        out_specs=pl.BlockSpec(memory_space=pl.ANY),
        scratch_shapes=[
            pltpu.VMEM((inner, group, block), jnp.bfloat16),
            pltpu.VMEM((SHIFTS, rows, block), jnp.float32),
            pltpu.VMEM((block, full), jnp.bfloat16),
            pltpu.VMEM((full, width), jnp.bfloat16),
            pltpu.VMEM((SHIFTS - 1, inner, group, block), jnp.bfloat16),
            pltpu.VMEM((count, 2) + (2,) * bits + (rows, half), jnp.float32),
            pltpu.VMEM((count, 2, block // 2 + UNIT_ROWS, half), jnp.bfloat16),
            pltpu.VMEM((count, 2, block // 2 + UNIT_ROWS, half), jnp.bfloat16),
            *hop_bufs,
            pltpu.SemaphoreType.DMA((chunks,)),
            pltpu.SemaphoreType.DMA((count,)),
            pltpu.SemaphoreType.DMA((SHIFTS - 1, chunks + 1)),
            pltpu.SemaphoreType.DMA((SHIFTS - 1, chunks + 1)),
            pltpu.SemaphoreType.DMA((count, 2, bits)),
            pltpu.SemaphoreType.DMA((count, 2, bits)),
        ],
        compiler_params=pltpu.CompilerParams(
            collective_id=0, has_side_effects=True, vmem_limit_bytes=58 * 2**20
        ),
        cost_estimate=pl.CostEstimate(
            flops=2 * SHIFTS * full * block * block,
            bytes_accessed=2 * full * block + 4 * SHIFTS * rows * block,
            transcendentals=0,
        ),
    )(flat)
    parts = 4 if rows % 32 == 0 else 1
    return pl.pallas_call(
        functools.partial(hand_on, parts),
        out_shape=jax.ShapeDtypeStruct(result.shape, result.dtype),
        in_specs=[pl.BlockSpec(memory_space=pl.ANY)],
        out_specs=pl.BlockSpec(memory_space=pl.ANY),
        scratch_shapes=[
            pltpu.VMEM(result.shape, result.dtype),
            pltpu.SemaphoreType.DMA((2, SHIFTS * parts)),
        ],
        compiler_params=pltpu.CompilerParams(vmem_limit_bytes=58 * 2**20),
        cost_estimate=pl.CostEstimate(
            flops=0, bytes_accessed=8 * SHIFTS * rows * block, transcendentals=0
        ),
    )(result)


def solution(mesh):
    n_aux, n_basis = mesh.shape["aux"], mesh.shape["basis"]
    return jax.shard_map(
        functools.partial(on_device, n_aux, n_basis),
        mesh=mesh,
        in_specs=(P("aux", None, "basis"),),
        out_specs=P(None, ("basis", "aux"), None),
        check_vma=False,
    )
```

```python
import functools

import jax
import jax.numpy as jnp
from jax import lax
from jax.experimental import pallas as pl
from jax.experimental.pallas import tpu as pltpu
from jax.sharding import PartitionSpec as P

SHIFTS = 3
SMALLEST = 2.0**-125
UNIT_ROWS = 16
MESH = pl.DeviceIdType.MESH


def round_up(value, step):
    return -(-value // step) * step


def encode(value, unit):
    scaled = value * (1.0 / unit)
    power = scaled * scaled
    power = power * power
    power = power * power
    return jnp.where(scaled < 0, -power, power).astype(jnp.bfloat16)


def decode(code, unit):
    code = code.astype(jnp.float32)
    fourth = lax.rsqrt(lax.rsqrt(jnp.maximum(jnp.abs(code), SMALLEST)))
    root = fourth * lax.rsqrt(fourth)
    root = jnp.where(code > 0, root, jnp.where(code < 0, -root, 0.0))
    return root * unit


def kernel(cfg, x_hbm, out_hbm, x_ref, out_ref, own_t, rhs, got, part, code_out, code_in, *rest):
    inner, group, full, block, width, chunks, bits, n_aux, n_basis = cfg
    depth = inner * group
    later = bits - 1
    hop_refs = rest[: 2 * later]
    load_sem, store_sem, ring_send, ring_recv, hop_send, hop_recv = rest[2 * later :]
    half = width // 2
    rows = block // n_aux
    me_aux = lax.axis_index("aux")
    me_basis = lax.axis_index("basis")
    left = lax.rem(me_basis + n_basis - 1, n_basis)
    right = lax.rem(me_basis + 1, n_basis)
    my_bit = [lax.rem(me_aux // (2**q), 2) for q in range(bits)]
    partner = [me_aux + (1 - 2 * my_bit[q]) * 2**q for q in range(bits)]

    def load(j):
        here = (slice(None), slice(None), pl.ds(j * width, width))
        return pltpu.make_async_copy(x_hbm.at[here], x_ref.at[here], load_sem.at[j])

    for j in range(chunks):
        load(j).start()

    barrier = pltpu.get_barrier_semaphore()
    for who in [{"basis": left}, {"basis": right}] + [{"aux": p} for p in partner]:
        pl.semaphore_signal(barrier, inc=1, device_id=who, device_id_type=MESH)
    if full > depth:
        rhs[depth:full, :] = jnp.zeros((full - depth, width), rhs.dtype)
    pl.semaphore_wait(barrier, 2 + bits)

    def ring_copy(s, j, low=0, high=inner):
        cols = pl.ds(j * width, width)
        source = x_ref if s == 0 else got.at[s - 1]
        return pltpu.make_async_remote_copy(
            src_ref=source.at[pl.ds(low, high - low), :, cols],
            dst_ref=got.at[s, pl.ds(low, high - low), :, cols],
            send_sem=ring_send.at[s, j if low == 0 else chunks],
            recv_sem=ring_recv.at[s, j if low == 0 else chunks],
            device_id={"basis": left},
            device_id_type=MESH,
        )

    def order(side):
        return list(range(bits)) if side == 0 else list(range(bits))[::-1]

    def cut(side, hop, last):
        index = [pl.ds(0, 2)] * bits
        for step, q in enumerate(order(side)[: hop + 1]):
            index[bits - 1 - q] = my_bit[q] if step < hop or not last else 1 - my_bit[q]
        return tuple(index)

    def hop_copy(n, side, hop):
        q = order(side)[hop]
        if hop == 0:
            source, target = code_out.at[n, side], code_in.at[n, side]
        else:
            source = part.at[(n, side) + cut(side, hop, True)]
            target = hop_refs[side * later + hop - 1].at[n]
        return pltpu.make_async_remote_copy(
            src_ref=source,
            dst_ref=target,
            send_sem=hop_send.at[n, side, hop],
            recv_sem=hop_recv.at[n, side, hop],
            device_id={"aux": partner[q]},
            device_id_type=MESH,
        )

    for j in range(chunks):
        load(j).wait()
        ring_copy(0, j).start()

    def flatten(s, j, low=0, high=inner):
        source = x_ref if s == 0 else got.at[s - 1]
        chunk = source[low:high, :, j * width : (j + 1) * width]
        chunk = chunk.reshape((high - low) * group, width)
        rhs[low * group : high * group, :] = chunk

    for j in range(chunks):
        flatten(0, j)
        own_t[j * width : (j + 1) * width, :] = rhs[...].T

    tiles = [(s, j) for s in range(SHIFTS) for j in range(chunks)]
    lhs_rows = min(256, block)
    sent = block // 2
    middle = round_up(depth * 7 // 8 - 128, 256) // group

    def multiply(n, low, high, add):
        def body(i, most):
            here = pl.ds(pl.multiple_of(i * lhs_rows, lhs_rows), lhs_rows)
            product = jnp.dot(
                own_t[here, low:high],
                rhs[low:high, :],
                preferred_element_type=jnp.float32,
            )
            per = lhs_rows // rows
            for r in range(per):
                g = i * per + r
                index = [lax.rem(g // (2**q), 2) for q in range(bits)][::-1]
                for side in range(2):
                    place = (n, side) + tuple(index)
                    value = product[
                        r * rows : (r + 1) * rows, side * half : (side + 1) * half
                    ]
                    if add:
                        value = value + part[place]
                    part[place] = value
                    size = jnp.abs(value).reshape(rows // 8, 8, half)
                    most = jnp.maximum(most, jnp.max(size, axis=0))
            return most

        start = jnp.zeros((8, half), jnp.float32)
        return lax.fori_loop(0, block // lhs_rows, body, start)

    def send_first(n, most):
        most = jnp.max(most)
        unit = jnp.maximum(most, 2.0**-90) * 2.0**-14
        for side in range(2):
            tail = (n, side, pl.ds(sent, UNIT_ROWS))
            code_out[tail] = jnp.full((UNIT_ROWS, half), unit).astype(jnp.bfloat16)
            used = code_out[tail].astype(jnp.float32)[0:1]
            value = part[(n, side) + cut(side, 0, True)].reshape(sent, half)
            code_out[n, side, 0:sent] = encode(value, used)
            hop_copy(n, side, 0).start()

    def store(n):
        s, j = tiles[n]
        here = (s, slice(None), pl.ds(j * width, width))
        return pltpu.make_async_copy(out_ref.at[here], out_hbm.at[here], store_sem.at[n])

    def finish(n, hop):
        s, j = tiles[n]
        for side in range(2):
            hop_copy(n, side, hop).wait_recv()
            index = (n, side) + cut(side, hop, False)
            if hop == 0:
                unit = code_in[n, side, sent:].astype(jnp.float32)[0:1]
                arrived = decode(code_in[n, side, 0:sent], unit)
                arrived = arrived.reshape((2,) * (bits - 1) + (rows, half))
            else:
                arrived = hop_refs[side * later + hop - 1][n]
            total = part[index] + arrived
            if hop < bits - 1:
                part[index] = total
                hop_copy(n, side, hop + 1).start()
            else:
                out_ref[s, :, j * width + side * half : j * width + (side + 1) * half] = total
        if hop == bits - 1:
            store(n).start()

    count = len(tiles)
    done = {}

    def catch_up(last, lag):
        for hop in range(bits):
            for m in range(done.get(hop, 0), max(last - lag * hop + 1, 0)):
                finish(m, hop)
                done[hop] = m + 1

    for n in range(count):
        s, j = tiles[n]
        split = n == count - 1
        if s > 0:
            if s == SHIFTS - 1:
                catch_up(n - 1, 0)
            ring_copy(s - 1, j, 0, middle if split else inner).wait_recv()
            if s == SHIFTS - 2 and j == chunks - 1:
                ring_copy(s, j, 0, middle).start()
                ring_copy(s, j, middle, inner).start()
            elif s < SHIFTS - 1:
                ring_copy(s, j).start()
        if split:
            flatten(s, j, 0, middle)
            multiply(n, 0, middle * group, False)
            ring_copy(s - 1, j, middle, inner).wait_recv()
            flatten(s, j, middle, inner)
            send_first(n, multiply(n, middle * group, full, True))
        else:
            flatten(s, j)
            send_first(n, multiply(n, 0, full, False))
        catch_up(n - 1, 1)
    catch_up(count - 1, 0)

    for s in range(SHIFTS - 1):
        for j in range(chunks):
            if (s, j) == (SHIFTS - 2, chunks - 1):
                ring_copy(s, j, 0, middle).wait_send()
                ring_copy(s, j, middle, inner).wait_send()
            else:
                ring_copy(s, j).wait_send()
    for n in range(count):
        store(n).wait()
    for n in range(count):
        for side in range(2):
            for hop in range(bits):
                hop_copy(n, side, hop).wait_send()


def hand_on(parts, source, target, held, sems):
    per = source.shape[1] // parts
    pairs = []
    for s in range(SHIFTS):
        for i in range(parts):
            here, k = (s, pl.ds(i * per, per)), s * parts + i
            into = pltpu.make_async_copy(source.at[here], held.at[here], sems.at[0, k])
            out = pltpu.make_async_copy(held.at[here], target.at[here], sems.at[1, k])
            pairs.append((into, out))
    for into, _ in pairs:
        into.start()
    for into, out in pairs:
        into.wait()
        out.start()
    for _, out in pairs:
        out.wait()


def on_device(n_aux, n_basis, factors):
    group, inner = factors.shape[0], factors.shape[1]
    depth = inner * group
    block = factors.shape[2]
    full = round_up(depth, 256)
    flat = jnp.transpose(factors, (1, 0, 2))
    bits = n_aux.bit_length() - 1
    width = 256
    chunks = block // width
    count = SHIFTS * chunks
    rows = block // n_aux
    half = width // 2
    hop_bufs = []
    for side in range(2):
        for hop in range(1, bits):
            shape = (count,) + (2,) * (bits - 1 - hop) + (rows, half)
            hop_bufs.append(pltpu.VMEM(shape, jnp.float32))
    cfg = (inner, group, full, block, width, chunks, bits, n_aux, n_basis)
    result = pl.pallas_call(
        functools.partial(kernel, cfg),
        out_shape=jax.ShapeDtypeStruct((SHIFTS, rows, block), jnp.float32),
        in_specs=[pl.BlockSpec(memory_space=pl.ANY)],
        out_specs=pl.BlockSpec(memory_space=pl.ANY),
        scratch_shapes=[
            pltpu.VMEM((inner, group, block), jnp.bfloat16),
            pltpu.VMEM((SHIFTS, rows, block), jnp.float32),
            pltpu.VMEM((block, full), jnp.bfloat16),
            pltpu.VMEM((full, width), jnp.bfloat16),
            pltpu.VMEM((SHIFTS - 1, inner, group, block), jnp.bfloat16),
            pltpu.VMEM((count, 2) + (2,) * bits + (rows, half), jnp.float32),
            pltpu.VMEM((count, 2, block // 2 + UNIT_ROWS, half), jnp.bfloat16),
            pltpu.VMEM((count, 2, block // 2 + UNIT_ROWS, half), jnp.bfloat16),
            *hop_bufs,
            pltpu.SemaphoreType.DMA((chunks,)),
            pltpu.SemaphoreType.DMA((count,)),
            pltpu.SemaphoreType.DMA((SHIFTS - 1, chunks + 1)),
            pltpu.SemaphoreType.DMA((SHIFTS - 1, chunks + 1)),
            pltpu.SemaphoreType.DMA((count, 2, bits)),
            pltpu.SemaphoreType.DMA((count, 2, bits)),
        ],
        compiler_params=pltpu.CompilerParams(
            collective_id=0, has_side_effects=True, vmem_limit_bytes=58 * 2**20
        ),
        cost_estimate=pl.CostEstimate(
            flops=2 * SHIFTS * full * block * block,
            bytes_accessed=2 * full * block + 4 * SHIFTS * rows * block,
            transcendentals=0,
        ),
    )(flat)
    parts = 4 if rows % 32 == 0 else 1
    return pl.pallas_call(
        functools.partial(hand_on, parts),
        out_shape=jax.ShapeDtypeStruct(result.shape, result.dtype),
        in_specs=[pl.BlockSpec(memory_space=pl.ANY)],
        out_specs=pl.BlockSpec(memory_space=pl.ANY),
        scratch_shapes=[
            pltpu.VMEM(result.shape, result.dtype),
            pltpu.SemaphoreType.DMA((2, SHIFTS * parts)),
        ],
        compiler_params=pltpu.CompilerParams(vmem_limit_bytes=58 * 2**20),
        cost_estimate=pl.CostEstimate(
            flops=0, bytes_accessed=8 * SHIFTS * rows * block, transcendentals=0
        ),
    )(result)


def solution(mesh):
    n_aux, n_basis = mesh.shape["aux"], mesh.shape["basis"]
    return jax.shard_map(
        functools.partial(on_device, n_aux, n_basis),
        mesh=mesh,
        in_specs=(P("aux", None, "basis"),),
        out_specs=P(None, ("basis", "aux"), None),
        check_vma=False,
    )
```
